1024 devices in a mesh: row: 64 (over z, x), col: 16 (over y, core).
Axes of the slice: x: 8, y: 8, z: 8, core: 2. Of those that a mesh axis runs over, the one named last changes fastest.
Arguments:
- a_tiles: bfloat16 [256, 48, 5, 128, 128], P('row', 'col'), may hold values from -0.25 to 0.25
- p_tiles: bfloat16 [256, 48, 2, 128, 128], P('row', 'col'), may hold values from -0.5 to 0.5
- c_slot: int32 [256, 48, 2, 5, 2], P('row', 'col'), may hold values from 0 to 95, as said below
Outputs:
- coarse: float32 [6144, 128, 128], P(('row', 'col'))
The draws below stay inside these ranges and needn't reach their ends.
Inputs may be any that keep to these rules, and one draw needn't show every extreme that they name: `c_slot`: each tile of a fine block belongs to an aggregate I of its grid row of devices, owned by owner I // 2, where owner o holds coarse tiles o * 6 to (o + 1) * 6 - 1. A term's label is owner(I) * 6 + 3 (I mod 2) + 0, 1 or 2, as the aggregate J of the neighbour tile is I itself, another aggregate of the same owner, or an aggregate of another owner (outside the grid J is I). The tiles of fine blocks on device column j belong to aggregates of owners j - 1, j or j + 1 only, so a device's terms land only in tiles of those owners.
All inputs are finite; a program needn't handle non-finite values.
Results may differ from the reference program's by a relative error of at most 0.0029.
Values may be sent and summed in bfloat16 or wider, within the bound.
A program may use at most 128 MiB of HBM per device.

```python
import jax
import jax.numpy as jnp
from jax import lax

B = 128
KP = 2
FBR = 4
FBC = 3
APO = 2
CTD = 6
GR = 256
GC = 48
SLOTS = 96
N_ROW = 64
N_COL = 16


def draw_c_slot(key, part):
    key = jax.random.fold_in(key, 7)
    key_one, key_two, key_three = jax.random.split(key, 3)
    columns = jnp.arange(GC, dtype=jnp.int32)
    device_col = columns // FBC
    left_ok = (columns % FBC == 0) & (device_col > 0)
    right_ok = (columns % FBC == FBC - 1) & (device_col < N_COL - 1)
    left_ok = left_ok[None, :, None]
    right_ok = right_ok[None, :, None]
    crossing = jax.random.randint(key_one, (GR, GC, KP), 0, 2)
    side = jax.random.randint(key_two, (GR, GC, KP), 0, 2)
    both_way = jnp.where(left_ok & right_ok, 2 * side - 1, jnp.where(left_ok, -1, jnp.where(right_ok, 1, 0)))
    moved = jnp.where(crossing == 1, both_way, 0)
    owner = device_col[None, :, None] + moved
    local = jax.random.randint(key_three, (GR, GC, KP), 0, APO)
    aggregate = (owner * APO + local).astype(jnp.int32)
    last_col = FBC * (N_COL - 1)
    aggregate = aggregate.at[0, 0, 0].set(0)
    aggregate = aggregate.at[0, last_col, 0].set(N_COL * APO - 1)
    aggregate = aggregate.at[0, last_col - 1, 0].set((N_COL - 2) * APO)
    padded = jnp.pad(aggregate, ((1, 1), (1, 1), (0, 0)), constant_values=-1)
    inner = padded[1:-1, 1:-1]
    beside = jnp.stack([inner, padded[:-2, 1:-1], padded[2:, 1:-1], padded[1:-1, :-2], padded[1:-1, 2:]], axis=2)
    first_agg = jnp.broadcast_to(aggregate[:, :, :, None, None], (GR, GC, KP, 5, KP))
    second_agg = jnp.broadcast_to(beside[:, :, None, :, :], (GR, GC, KP, 5, KP))
    second_agg = jnp.where(second_agg < 0, first_agg, second_agg)
    first_owner = first_agg // APO
    kind = jnp.where(second_agg == first_agg, 0, jnp.where(second_agg // APO == first_owner, 1, 2))
    labels = first_owner * CTD + 3 * (first_agg % APO) + kind
    return labels.astype(jnp.int32)


def steps_of(stream_key, shape, cuts, low, high):
    factor_of, own = 1.0, jax.random.fold_in(stream_key, 6)
    for axis_at, blocks in cuts:
        draws = jnp.exp(jax.random.uniform(jax.random.fold_in(own, axis_at), (blocks,), jnp.float32, low / len(cuts), high / len(cuts)))
        factor_of = factor_of * jnp.repeat(draws, shape[axis_at] // blocks).reshape([-1 if axis == axis_at else 1 for axis in range(len(shape))])
    return factor_of


def normal_values(rng, dims, deviation, bound, shards=(), kind=jnp.bfloat16):
    drawn = jax.random.normal(rng, dims, jnp.float32) * deviation
    if len(shards) > 0:
        drawn = steps_of(rng, dims, shards, -0.22, 0.18) * drawn
    return jnp.clip(drawn, min=-bound, max=bound).astype(kind)


def setup_inputs(seed: int = 0) -> dict:
    key_of = jax.random.split(jax.random.key(seed), 4)
    a_tiles = normal_values(key_of[0], (GR, GC, 5, B, B), (5 * B) ** -0.5, 0.25, ((0, 64), (1, 16)))
    p_tiles = normal_values(key_of[1], (GR, GC, KP, B, B), B ** -0.5, 0.5, ((0, 64), (1, 16)))
    c_slot = draw_c_slot(jax.random.fold_in(key_of[3], 71), 0)
    return {"a_tiles": a_tiles, "p_tiles": p_tiles, "c_slot": c_slot}


def reference(a_tiles, p_tiles, c_slot):
    p_pad = jnp.pad(p_tiles, ((1, 1), (1, 1), (0, 0), (0, 0), (0, 0)))

    def group(index):
        first = (index * FBR).astype(jnp.int32)
        a_rows = lax.dynamic_slice_in_dim(a_tiles, first, FBR, 0)
        p_rows = lax.dynamic_slice_in_dim(p_pad, first, FBR + 2, 0)
        own = p_rows[1:-1, 1:-1]
        near = jnp.stack([own, p_rows[:-2, 1:-1], p_rows[2:, 1:-1], p_rows[1:-1, :-2], p_rows[1:-1, 2:]], axis=2)
        ap_tiles = jnp.einsum("xykij,xykqjl->xykqil", a_rows.astype(jnp.float32), near.astype(jnp.float32)).astype(jnp.bfloat16)
        terms = jnp.einsum("xypji,xykqjl->xypkqil", own.astype(jnp.float32), ap_tiles.astype(jnp.float32))
        labels = lax.dynamic_slice_in_dim(c_slot, first, FBR, 0)
        return jax.ops.segment_sum(terms.reshape(-1, B, B), labels.reshape(-1), num_segments=SLOTS)

    parts = lax.map(group, jnp.arange(N_ROW, dtype=jnp.int32))
    return parts.reshape(N_ROW * SLOTS, B, B)
```

```python
import functools

import jax
import jax.numpy as jnp
from jax import lax
from jax.experimental import pallas as pl
from jax.experimental.pallas import tpu as pltpu
from jax.sharding import PartitionSpec as P

MESH = pl.DeviceIdType.MESH
B = 128
KP = 2
FBR = 4
FBC = 3
CTD = 6
SELF, ABOVE, BELOW, LEFT, RIGHT = range(5)
F32, BF16 = jnp.float32, jnp.bfloat16


def place(r):
    return {1: (0, 0), 2: (0, 1), 0: (1, 0), 3: (1, 1)}[r]


def kernel(n_row, n_col, a_hbm, p_hbm, slot_hbm, mine_hbm, far_hbm, near_hbm, slot, a_v, p_v, acc, pt, g, part, mine_v, out_v,
           load_sem, halo_send, halo_recv, part_send, part_recv, store_sem):
    row, col = lax.axis_index("row"), lax.axis_index("col")
    odd = lax.rem(col, 2)
    far, near = col - 1 + 2 * odd, col + 1 - 2 * odd
    has_above, has_below = row > 0, row < n_row - 1
    has_far = jnp.logical_and(far >= 0, far < n_col)
    to_far, to_near = 2 * odd - 1, 1 - 2 * odd

    barrier = pltpu.get_barrier_semaphore()

    def greet(there):
        pl.semaphore_signal(barrier, inc=1, device_id=there, device_id_type=MESH)

    pl.when(has_above)(lambda: greet((row - 1, col)))
    pl.when(has_below)(lambda: greet((row + 1, col)))
    pl.when(has_far)(lambda: greet((row, far)))
    greet((row, near))

    load_p = pltpu.make_async_copy(p_hbm, p_v.at[pl.ds(1, FBR), pl.ds(1, FBC)], load_sem.at[0])
    load_a = pltpu.make_async_copy(a_hbm, a_v, load_sem.at[1])
    load_slot = pltpu.make_async_copy(slot_hbm, slot, load_sem.at[2])
    load_p.start()
    load_slot.start()
    load_a.start()

    def halo(index, source, target, there):
        return pltpu.make_async_remote_copy(
            src_ref=source, dst_ref=target, send_sem=halo_send.at[index], recv_sem=halo_recv.at[index],
            device_id=there, device_id_type=MESH)

    rim_above = p_v.at[0, pl.ds(1, FBC)]
    rim_below = p_v.at[FBR + 1, pl.ds(1, FBC)]

    def rim_column(at):
        return p_v.at[pl.ds(1, FBR), at]

    up = halo(0, p_hbm.at[0], rim_below, (row - 1, col))
    down = halo(1, p_hbm.at[FBR - 1], rim_above, (row + 1, col))
    across = halo(2, p_hbm.at[:, (FBC - 1) * odd], rim_column((FBC + 1) * (1 - odd)), (row, far))
    beside = halo(3, p_hbm.at[:, (FBC - 1) * (1 - odd)], rim_column((FBC + 1) * odd), (row, near))
    up_in = halo(0, p_hbm.at[0], rim_below, (row - 1, col))
    down_in = halo(1, p_hbm.at[0], rim_above, (row + 1, col))
    across_in = halo(2, p_hbm.at[:, 0], rim_column((FBC + 1) * odd), (row, far))
    beside_in = halo(3, p_hbm.at[:, 0], rim_column((FBC + 1) * (1 - odd)), (row, near))

    count = 1 + has_above.astype(jnp.int32) + has_below.astype(jnp.int32) + has_far.astype(jnp.int32)
    pl.semaphore_wait(barrier, count)
    pl.when(has_above)(up.start)
    pl.when(has_below)(down.start)
    pl.when(has_far)(across.start)
    beside.start()

    @pl.when(jnp.logical_not(has_above))
    def _():
        rim_above[...] = jnp.zeros(rim_above.shape, BF16)

    @pl.when(jnp.logical_not(has_below))
    def _():
        rim_below[...] = jnp.zeros(rim_below.shape, BF16)

    @pl.when(jnp.logical_not(has_far))
    def _():
        edge = (FBC + 1) * odd
        for r in range(FBR):
            p_v[1 + r, edge] = jnp.zeros((KP, B, B), BF16)

    load_slot.wait()
    load_p.wait()

    def transpose_half(half, carry):
        for i in range(2):
            r = (1 - half) * (1 + i) + half * 3 * i
            for c in range(FBC):
                for p in range(KP):
                    turned = p_v[1 + r, 1 + c, p].T
                    label = slot[r, c, p, p, SELF] - col * CTD
                    at = ((i * FBC + c) * KP + p) * B
                    for o, shift in enumerate((to_far, to_near, 0)):
                        for aggregate in range(2):
                            keep = jnp.where(label == shift * CTD + 3 * aggregate, 1.0, 0.0)
                            pt[o, half, aggregate * B : (aggregate + 1) * B, at : at + B] = turned * keep.astype(BF16)
        return carry

    lax.fori_loop(0, 2, transpose_half, 0)

    def products(r, c, k, rim_r, rim_c):
        right = jnp.concatenate([p_v[rim_r, rim_c, 0], p_v[rim_r, rim_c, 1]], axis=1)
        ap = jnp.dot(a_v[r, c, k], right, preferred_element_type=F32).astype(BF16).astype(F32)
        tiles = [ap[:, :B], ap[:, B:]]
        sums = [tiles[0] + tiles[1]]
        for p in range(KP):
            base = slot[r, c, p, p, SELF]
            for kind in range(2):
                keep = [jnp.where(slot[r, c, p, q, k] == base + kind, 1.0, 0.0) for q in range(KP)]
                sums.append(tiles[0] * keep[0] + tiles[1] * keep[1])
        return sums

    def add(one, other):
        return [x + y for x, y in zip(one, other)]

    def held(r, c):
        return [acc[r, c, n] for n in range(5)]

    def hold(r, c, sums):
        for n in range(5):
            acc[r, c, n] = sums[n]

    def finish(r, c, sums):
        half, i = place(r)
        for p in range(KP):
            first, second = sums[1 + 2 * p], sums[2 + 2 * p]
            at = ((i * FBC + c) * KP + p) * B
            g[half, at : at + B, :B] = first.astype(BF16)
            g[half, at : at + B, B : 2 * B] = second.astype(BF16)
            g[half, at : at + B, 2 * B :] = (sums[0] - first - second).astype(BF16)

    load_a.wait()

    def within_row(r, carry):
        for c in range(FBC):
            sums = products(r, c, SELF, r + 1, c + 1)
            if c > 0:
                sums = add(sums, products(r, c, LEFT, r + 1, c))
            if c < FBC - 1:
                sums = add(sums, products(r, c, RIGHT, r + 1, c + 2))
            hold(r, c, sums)
        return carry

    lax.fori_loop(0, FBR, within_row, 0)

    def between_rows(r, carry):
        for c in range(FBC):
            hold(r, c, add(held(r, c), products(r, c, BELOW, r + 2, c + 1)))
            hold(r + 1, c, add(held(r + 1, c), products(r + 1, c, ABOVE, r + 1, c + 1)))
        return carry

    lax.fori_loop(0, FBR - 1, between_rows, 0)

    beside_in.wait_recv()
    pl.when(has_far)(across_in.wait_recv)

    for r in range(FBR):
        left = add(held(r, 0), products(r, 0, LEFT, r + 1, 0))
        right = add(held(r, FBC - 1), products(r, FBC - 1, RIGHT, r + 1, FBC + 1))
        if r in (1, 2):
            finish(r, 0, left)
            finish(r, 1, held(r, 1))
            finish(r, 2, right)
        else:
            hold(r, 0, left)
            hold(r, FBC - 1, right)

    def first_half(o, carry):
        part[o] = jnp.dot(pt[o, 0], g[0], preferred_element_type=F32)
        return carry

    lax.fori_loop(0, 3, first_half, 0)

    pl.when(has_above)(down_in.wait_recv)
    pl.when(has_below)(up_in.wait_recv)
    for c in range(FBC):
        finish(0, c, add(held(0, c), products(0, c, ABOVE, 0, c + 1)))
        finish(FBR - 1, c, add(held(FBR - 1, c), products(FBR - 1, c, BELOW, FBR + 1, c + 1)))

    def partial_tiles(o, target):
        total = part[o] + jnp.dot(pt[o, 1], g[1], preferred_element_type=F32)
        for aggregate in range(2):
            for kind in range(3):
                tile = total[aggregate * B : (aggregate + 1) * B, kind * B : (kind + 1) * B]
                target[3 * aggregate + kind] = tile.astype(target.dtype)

    def partial(index, target, there):
        return pltpu.make_async_remote_copy(
            src_ref=out_v.at[index], dst_ref=target, send_sem=part_send.at[index], recv_sem=part_recv.at[index],
            device_id=there, device_id_type=MESH)

    to_far_copy = partial(0, far_hbm, (row, far))
    to_near_copy = partial(1, near_hbm, (row, near))
    partial_tiles(0, out_v.at[0])
    pl.when(has_far)(to_far_copy.start)

    @pl.when(jnp.logical_not(has_far))
    def _():
        out_v[0] = jnp.zeros((CTD, B, B), BF16)
        fill = pltpu.make_async_copy(out_v.at[0], far_hbm, store_sem.at[1])
        fill.start()
        fill.wait()

    partial_tiles(1, out_v.at[1])
    to_near_copy.start()
    partial_tiles(2, mine_v)
    store = pltpu.make_async_copy(mine_v, mine_hbm, store_sem.at[0])
    store.start()

    pl.when(has_above)(up.wait_send)
    pl.when(has_below)(down.wait_send)
    pl.when(has_far)(across.wait_send)
    beside.wait_send()
    to_near_copy.wait()
    store.wait()
    pl.when(has_far)(to_far_copy.wait)


def body(n_row, n_col, a_tiles, p_tiles, c_slot):
    any_space, hbm = pl.BlockSpec(memory_space=pl.ANY), pl.BlockSpec(memory_space=pltpu.HBM)
    mine, far, near = pl.pallas_call(
        functools.partial(kernel, n_row, n_col),
        out_shape=[
            jax.ShapeDtypeStruct((CTD, B, B), F32),
            jax.ShapeDtypeStruct((CTD, B, B), BF16),
            jax.ShapeDtypeStruct((CTD, B, B), BF16),
        ],
        in_specs=[hbm, hbm, hbm],
        out_specs=[any_space] * 3,
        scratch_shapes=[
            pltpu.SMEM((FBR, FBC, KP, KP, 5), jnp.int32),
            pltpu.VMEM((FBR, FBC, 5, B, B), BF16),
            pltpu.VMEM((FBR + 2, FBC + 2, KP, B, B), BF16),
            pltpu.VMEM((FBR, FBC, 5, B, B), F32),
            pltpu.VMEM((3, 2, 2 * B, 2 * FBC * KP * B), BF16),
            pltpu.VMEM((2, 2 * FBC * KP * B, 3 * B), BF16),
            pltpu.VMEM((3, 2 * B, 3 * B), F32),
            pltpu.VMEM((CTD, B, B), F32),
            pltpu.VMEM((2, CTD, B, B), BF16),
            pltpu.SemaphoreType.DMA((3,)),
            pltpu.SemaphoreType.DMA((4,)),
            pltpu.SemaphoreType.DMA((4,)),
            pltpu.SemaphoreType.DMA((2,)),
            pltpu.SemaphoreType.DMA((2,)),
            pltpu.SemaphoreType.DMA((2,)),
        ],
        compiler_params=pltpu.CompilerParams(
            collective_id=0, has_side_effects=True, vmem_limit_bytes=48 * 1024 * 1024),
        name="coarse",
    )(a_tiles, p_tiles, jnp.swapaxes(c_slot, 3, 4))
    return mine + far.astype(F32) + near.astype(F32)


def solution(mesh):
    spec = P("row", "col", None, None, None)
    return jax.shard_map(
        functools.partial(body, mesh.shape["row"], mesh.shape["col"]), mesh=mesh, in_specs=(spec, spec, spec),
        out_specs=P(("row", "col"), None, None), check_vma=False)
```

```python
import functools

import jax
import jax.numpy as jnp
from jax import lax
from jax.experimental import pallas as pl
from jax.experimental.pallas import tpu as pltpu
from jax.sharding import PartitionSpec as P

MESH = pl.DeviceIdType.MESH
B = 128
KP = 2
FBR = 4
FBC = 3
CTD = 6
SELF, ABOVE, BELOW, LEFT, RIGHT = range(5)
F32, BF16 = jnp.float32, jnp.bfloat16


def kernel(n_row, n_col, a_hbm, p_hbm, slot_hbm, mine, far_hbm, near_hbm, slot, a_v, p_v, acc, pt, chain, out_v,
           load_sem, halo_send, halo_recv, part_send, part_recv, fill_sem):
    row, col = lax.axis_index("row"), lax.axis_index("col")
    odd = lax.rem(col, 2)
    far, near = col - 1 + 2 * odd, col + 1 - 2 * odd
    has_above, has_below = row > 0, row < n_row - 1
    has_far = jnp.logical_and(far >= 0, far < n_col)

    barrier = pltpu.get_barrier_semaphore()

    def greet(there):
        pl.semaphore_signal(barrier, inc=1, device_id=there, device_id_type=MESH)

    pl.when(has_above)(lambda: greet((row - 1, col)))
    pl.when(has_below)(lambda: greet((row + 1, col)))
    pl.when(has_far)(lambda: greet((row, far)))

    load_slot = pltpu.make_async_copy(slot_hbm, slot, load_sem.at[2 * FBR])
    load_slot.start()

    def load_p(r):
        return pltpu.make_async_copy(p_hbm.at[r], p_v.at[1 + r, pl.ds(1, FBC)], load_sem.at[FBR + r])

    def load_a(r):
        return pltpu.make_async_copy(a_hbm.at[r], a_v.at[r], load_sem.at[r])

    for r in range(FBR):
        load_p(r).start()
    for r in range(FBR):
        load_a(r).start()

    def halo(index, source, target, there):
        return pltpu.make_async_remote_copy(
            src_ref=source, dst_ref=target, send_sem=halo_send.at[index], recv_sem=halo_recv.at[index],
            device_id=there, device_id_type=MESH)

    rim_above = p_v.at[0, pl.ds(1, FBC)]
    rim_below = p_v.at[FBR + 1, pl.ds(1, FBC)]

    def rim_column(at):
        return p_v.at[pl.ds(1, FBR), at]

    up = halo(0, p_hbm.at[0], rim_below, (row - 1, col))
    down = halo(1, p_hbm.at[FBR - 1], rim_above, (row + 1, col))
    across = halo(2, p_hbm.at[:, (FBC - 1) * odd], rim_column((FBC + 1) * (1 - odd)), (row, far))
    beside = halo(3, p_hbm.at[:, (FBC - 1) * (1 - odd)], rim_column((FBC + 1) * odd), (row, near))
    up_in = halo(0, p_hbm.at[0], rim_below, (row - 1, col))
    down_in = halo(1, p_hbm.at[0], rim_above, (row + 1, col))
    across_in = halo(2, p_hbm.at[:, 0], rim_column((FBC + 1) * odd), (row, far))
    beside_in = halo(3, p_hbm.at[:, 0], rim_column((FBC + 1) * (1 - odd)), (row, near))

    count = 1 - odd + has_above.astype(jnp.int32) + has_below.astype(jnp.int32) + has_far.astype(jnp.int32)
    pl.semaphore_wait(barrier, count)
    greet((row, near))
    pl.when(has_far)(across.start)
    pl.when(has_above)(up.start)
    pl.when(has_below)(down.start)
    pl.when(odd == 0)(beside.start)

    @pl.when(jnp.logical_not(has_above))
    def _():
        rim_above[...] = jnp.zeros(rim_above.shape, BF16)

    @pl.when(jnp.logical_not(has_below))
    def _():
        rim_below[...] = jnp.zeros(rim_below.shape, BF16)

    fill = pltpu.make_async_copy(out_v.at[1], far_hbm, fill_sem)

    @pl.when(jnp.logical_not(has_far))
    def _():
        edge = (FBC + 1) * odd
        for r in range(FBR):
            p_v[1 + r, edge] = jnp.zeros((KP, B, B), BF16)
        out_v[1] = jnp.zeros((CTD, B, B), BF16)
        fill.start()

    chain[0] = jnp.zeros((B, 3 * B), F32)
    def transpose_row(r, carry):
        load_p(r).wait()
        for c in range(FBC):
            for p in range(KP):
                pt[r, c, p] = p_v[1 + r, 1 + c, p].T
        return carry

    lax.fori_loop(0, FBR, transpose_row, 0)
    load_slot.wait()

    def products(r, c, k, rim_r, rim_c):
        right = jnp.concatenate([p_v[rim_r, rim_c, 0], p_v[rim_r, rim_c, 1]], axis=1)
        ap = jnp.dot(a_v[r, c, k], right, preferred_element_type=F32).astype(BF16).astype(F32)
        tiles = [ap[:, :B], ap[:, B:]]
        sums = [tiles[0] + tiles[1]]
        for p in range(KP):
            base = slot[r, c, p, p, SELF]
            for kind in range(2):
                keep = [jnp.where(slot[r, c, p, q, k] == base + kind, 1.0, 0.0) for q in range(KP)]
                sums.append(tiles[0] * keep[0] + tiles[1] * keep[1])
        return sums

    def add(one, other):
        return [x + y for x, y in zip(one, other)]

    def held(r, c):
        return [acc[r, c, n] for n in range(5)]

    def hold(r, c, sums):
        for n in range(5):
            acc[r, c, n] = sums[n]

    def gather(r, c, sums, last):
        for p in range(KP):
            first, second = sums[1 + 2 * p], sums[2 + 2 * p]
            kinds = jnp.concatenate([first, second, sums[0] - first - second], axis=1).astype(BF16)
            term = jnp.dot(pt[r, c, p], kinds, preferred_element_type=F32)
            label = slot[r, c, p, p, SELF] - (col - 1) * CTD
            at = 1 + (r * FBC + c) * KP + p
            before = jnp.int32(0)
            for n in range(6):
                before = jnp.where(label == 3 * n, last[n], before)
            last = [jnp.where(label == 3 * n, at, last[n]) for n in range(6)]
            chain[at] = term + chain[before]
        return last

    def within_row(r, carry):
        load_a(r).wait()
        for c in range(FBC):
            sums = products(r, c, SELF, r + 1, c + 1)
            if c > 0:
                sums = add(sums, products(r, c, LEFT, r + 1, c))
            if c < FBC - 1:
                sums = add(sums, products(r, c, RIGHT, r + 1, c + 2))
            hold(r, c, sums)
        return carry

    lax.fori_loop(0, FBR, within_row, 0)

    def between_rows(r, carry):
        for c in range(FBC):
            hold(r, c, add(held(r, c), products(r, c, BELOW, r + 2, c + 1)))
            hold(r + 1, c, add(held(r + 1, c), products(r + 1, c, ABOVE, r + 1, c + 1)))
        return carry

    lax.fori_loop(0, FBR - 1, between_rows, 0)

    @pl.when(odd == 1)
    def _():
        pl.semaphore_wait(barrier, 1)
        beside.start()

    beside_in.wait_recv()
    pl.when(has_far)(across_in.wait_recv)

    def along_row(r):
        left = add(held(r, 0), products(r, 0, LEFT, r + 1, 0))
        right = add(held(r, FBC - 1), products(r, FBC - 1, RIGHT, r + 1, FBC + 1))
        return left, right

    last = [jnp.int32(0)] * 6

    def inner_row(r, last):
        left, right = along_row(r)
        for c, sums in enumerate((left, held(r, 1), right)):
            last = gather(r, c, sums, last)
        return last

    last = lax.fori_loop(1, FBR - 1, inner_row, last)
    for r in (0, FBR - 1):
        left, right = along_row(r)
        hold(r, 0, left)
        hold(r, FBC - 1, right)

    pl.when(has_above)(down_in.wait_recv)
    pl.when(has_below)(up_in.wait_recv)
    for r, k, rim in ((0, ABOVE, 0), (FBR - 1, BELOW, FBR + 1)):
        for c in range(FBC):
            last = gather(r, c, add(held(r, c), products(r, c, k, rim, c + 1)), last)

    def partial_tiles(owner, target):
        for aggregate in range(2):
            total = chain[jnp.where(owner == -1, last[aggregate], jnp.where(owner == 0, last[2 + aggregate], last[4 + aggregate]))]
            for kind in range(3):
                target[3 * aggregate + kind] = total[:, kind * B : (kind + 1) * B].astype(target.dtype)

    def partial(index, target, there):
        return pltpu.make_async_remote_copy(
            src_ref=out_v.at[index], dst_ref=target, send_sem=part_send.at[index], recv_sem=part_recv.at[index],
            device_id=there, device_id_type=MESH)

    to_near_copy = partial(0, near_hbm, (row, near))
    to_far_copy = partial(1, far_hbm, (row, far))
    partial_tiles(near - col, out_v.at[0])
    to_near_copy.start()

    @pl.when(has_far)
    def _():
        partial_tiles(far - col, out_v.at[1])
        to_far_copy.start()

    partial_tiles(0, mine)

    pl.when(has_above)(up.wait_send)
    pl.when(has_below)(down.wait_send)
    pl.when(has_far)(across.wait_send)
    beside.wait_send()
    pl.when(jnp.logical_not(has_far))(fill.wait)
    to_near_copy.wait()
    pl.when(has_far)(to_far_copy.wait)


def body(n_row, n_col, a_tiles, p_tiles, c_slot):
    any_space, hbm = pl.BlockSpec(memory_space=pl.ANY), pl.BlockSpec(memory_space=pltpu.HBM)
    operands = [
        pltpu.with_memory_space_constraint(x, pltpu.HBM) for x in (a_tiles, p_tiles, jnp.swapaxes(c_slot, 3, 4))
    ]
    mine, far, near = pl.pallas_call(
        functools.partial(kernel, n_row, n_col),
        out_shape=[
            jax.ShapeDtypeStruct((CTD, B, B), F32),
            jax.ShapeDtypeStruct((CTD, B, B), BF16),
            jax.ShapeDtypeStruct((CTD, B, B), BF16),
        ],
        in_specs=[hbm, hbm, hbm],
        out_specs=[pl.BlockSpec(memory_space=pltpu.VMEM), any_space, any_space],
        scratch_shapes=[
            pltpu.SMEM((FBR, FBC, KP, KP, 5), jnp.int32),
            pltpu.VMEM((FBR, FBC, 5, B, B), BF16),
            pltpu.VMEM((FBR + 2, FBC + 2, KP, B, B), BF16),
            pltpu.VMEM((FBR, FBC, 5, B, B), F32),
            pltpu.VMEM((FBR, FBC, KP, B, B), BF16),
            pltpu.VMEM((1 + FBR * FBC * KP, B, 3 * B), F32),
            pltpu.VMEM((2, CTD, B, B), BF16),
            pltpu.SemaphoreType.DMA((2 * FBR + 1,)),
            pltpu.SemaphoreType.DMA((4,)),
            pltpu.SemaphoreType.DMA((4,)),
            pltpu.SemaphoreType.DMA((2,)),
            pltpu.SemaphoreType.DMA((2,)),
            pltpu.SemaphoreType.DMA,
        ],
        compiler_params=pltpu.CompilerParams(
            collective_id=0, has_side_effects=True, vmem_limit_bytes=48 * 1024 * 1024),
        name="coarse",
    )(*operands)
    return mine + far.astype(F32) + near.astype(F32)


def solution(mesh):
    spec = P("row", "col", None, None, None)
    return jax.shard_map(
        functools.partial(body, mesh.shape["row"], mesh.shape["col"]), mesh=mesh, in_specs=(spec, spec, spec),
        out_specs=P(("row", "col"), None, None), check_vma=False)
```

```python
import functools

import jax
import jax.numpy as jnp
from jax import lax
from jax.experimental import pallas as pl
from jax.experimental.pallas import tpu as pltpu
from jax.sharding import PartitionSpec as P

MESH = pl.DeviceIdType.MESH
B = 128
KP = 2
FBR = 4
FBC = 3
CTD = 6
SELF, ABOVE, BELOW, LEFT, RIGHT = range(5)
F32, BF16 = jnp.float32, jnp.bfloat16


def kernel(n_row, n_col, a_hbm, p_hbm, slot_hbm, mine, far_hbm, near_hbm, slot, a_v, p_v, acc, pt, chain, out_v,
           load_sem, halo_send, halo_recv, part_send, part_recv, fill_sem):
    row, col = lax.axis_index("row"), lax.axis_index("col")
    odd = lax.rem(col, 2)
    far, near = col - 1 + 2 * odd, col + 1 - 2 * odd
    has_above, has_below = row > 0, row < n_row - 1
    has_far = jnp.logical_and(far >= 0, far < n_col)

    barrier = pltpu.get_barrier_semaphore()

    def greet(there):
        pl.semaphore_signal(barrier, inc=1, device_id=there, device_id_type=MESH)

    pl.when(has_above)(lambda: greet((row - 1, col)))
    pl.when(has_below)(lambda: greet((row + 1, col)))
    pl.when(has_far)(lambda: greet((row, far)))

    load_slot = pltpu.make_async_copy(slot_hbm, slot, load_sem.at[2 * FBR])
    load_slot.start()

    def load_p(r):
        return pltpu.make_async_copy(p_hbm.at[r], p_v.at[1 + r, pl.ds(1, FBC)], load_sem.at[FBR + r])

    def load_a(r):
        return pltpu.make_async_copy(a_hbm.at[r], a_v.at[r], load_sem.at[r])

    for r in range(FBR):
        load_p(r).start()
    for r in (1, 2, 0, 3):
        load_a(r).start()

    def halo(index, source, target, there):
        return pltpu.make_async_remote_copy(
            src_ref=source, dst_ref=target, send_sem=halo_send.at[index], recv_sem=halo_recv.at[index],
            device_id=there, device_id_type=MESH)

    rim_above = p_v.at[0, pl.ds(1, FBC)]
    rim_below = p_v.at[FBR + 1, pl.ds(1, FBC)]

    def rim_column(at):
        return p_v.at[pl.ds(1, FBR), at]

    up = halo(0, p_hbm.at[0], rim_below, (row - 1, col))
    down = halo(1, p_hbm.at[FBR - 1], rim_above, (row + 1, col))
    across = halo(2, p_hbm.at[:, (FBC - 1) * odd], rim_column((FBC + 1) * (1 - odd)), (row, far))
    beside = halo(3, p_hbm.at[:, (FBC - 1) * (1 - odd)], rim_column((FBC + 1) * odd), (row, near))
    up_in = halo(0, p_hbm.at[0], rim_below, (row - 1, col))
    down_in = halo(1, p_hbm.at[0], rim_above, (row + 1, col))
    across_in = halo(2, p_hbm.at[:, 0], rim_column((FBC + 1) * odd), (row, far))
    beside_in = halo(3, p_hbm.at[:, 0], rim_column((FBC + 1) * (1 - odd)), (row, near))

    def meet():
        count = 1 - odd + has_above.astype(jnp.int32) + has_below.astype(jnp.int32) + has_far.astype(jnp.int32)
        pl.semaphore_wait(barrier, count)
        greet((row, near))
        pl.when(has_far)(across.start)
        pl.when(has_above)(up.start)
        pl.when(has_below)(down.start)
        pl.when(odd == 0)(beside.start)

    pl.when(row != 1)(meet)

    @pl.when(jnp.logical_not(has_above))
    def _():
        rim_above[...] = jnp.zeros(rim_above.shape, BF16)

    @pl.when(jnp.logical_not(has_below))
    def _():
        rim_below[...] = jnp.zeros(rim_below.shape, BF16)

    fill = pltpu.make_async_copy(out_v.at[1], far_hbm, fill_sem)

    @pl.when(jnp.logical_not(has_far))
    def _():
        edge = (FBC + 1) * odd
        for r in range(FBR):
            p_v[1 + r, edge] = jnp.zeros((KP, B, B), BF16)
        out_v[1] = jnp.zeros((CTD, B, B), BF16)
        fill.start()

    chain[0] = jnp.zeros((B, 3 * B), F32)
    def transpose_row(r, carry):
        load_p(r).wait()
        for c in range(FBC):
            for p in range(KP):
                pt[r, c, p] = p_v[1 + r, 1 + c, p].T
        return carry

    lax.fori_loop(0, FBR, transpose_row, 0)
    load_slot.wait()

    def products(r, c, k, rim_r, rim_c):
        right = jnp.concatenate([p_v[rim_r, rim_c, 0], p_v[rim_r, rim_c, 1]], axis=1)
        ap = jnp.dot(a_v[r, c, k], right, preferred_element_type=F32).astype(BF16).astype(F32)
        tiles = [ap[:, :B], ap[:, B:]]
        sums = [tiles[0] + tiles[1]]
        for p in range(KP):
            base = slot[r, c, p, p, SELF]
            for kind in range(2):
                if k is SELF:
                    other = tiles[1 - p] * jnp.where(slot[r, c, p, 1 - p, k] == base + kind, 1.0, 0.0)
                    sums.append(tiles[p] + other if kind == 0 else other)
                    continue
                keep = [jnp.where(slot[r, c, p, q, k] == base + kind, 1.0, 0.0) for q in range(KP)]
                sums.append(tiles[0] * keep[0] + tiles[1] * keep[1])
        return sums

    def add(one, other):
        return [x + y for x, y in zip(one, other)]

    def held(r, c):
        return [acc[r, c, n] for n in range(5)]

    def hold(r, c, sums):
        for n in range(5):
            acc[r, c, n] = sums[n]

    def gather(r, c, sums, last):
        for p in range(KP):
            first, second = sums[1 + 2 * p], sums[2 + 2 * p]
            kinds = jnp.concatenate([first, second, sums[0] - first - second], axis=1).astype(BF16)
            term = jnp.dot(pt[r, c, p], kinds, preferred_element_type=F32)
            label = slot[r, c, p, p, SELF] - (col - 1) * CTD
            at = 1 + (r * FBC + c) * KP + p
            before = jnp.int32(0)
            for n in range(6):
                before = jnp.where(label == 3 * n, last[n], before)
            last = [jnp.where(label == 3 * n, at, last[n]) for n in range(6)]
            chain[at] = term + chain[before]
        return last

    def interior(r, verticals):
        load_a(r).wait()
        for c in range(FBC):
            sums = products(r, c, SELF, r + 1, c + 1)
            if c > 0:
                sums = add(sums, products(r, c, LEFT, r + 1, c))
            if c < FBC - 1:
                sums = add(sums, products(r, c, RIGHT, r + 1, c + 2))
            for k, rim in verticals:
                sums = add(sums, products(r, c, k, rim, c + 1))
            hold(r, c, sums)

    def inner_interior(r, carry):
        interior(r, ((ABOVE, r), (BELOW, r + 2)))
        return carry

    def outer_interior(i, carry):
        interior((FBR - 1) * i, ((BELOW - i, 2 + i),))
        return carry

    lax.fori_loop(1, FBR - 1, inner_interior, 0)
    pl.when(row == 1)(meet)
    lax.fori_loop(0, 2, outer_interior, 0)

    first, final = 0, FBR - 1
    inner = range(1, FBR - 1)

    def with_side(r, c):
        k, rim = (LEFT, 0) if c == 0 else (RIGHT, FBC + 1)
        return add(held(r, c), products(r, c, k, r + 1, rim))

    def with_end(r, c):
        k, rim = (ABOVE, 0) if r == first else (BELOW, FBR + 1)
        return add(held(r, c), products(r, c, k, rim, c + 1))

    def hold_all(sums_of, blocks):
        for r, c in blocks:
            hold(r, c, sums_of(r, c))

    def gather_all(sums_of, blocks, last):
        for r, c in blocks:
            last = gather(r, c, sums_of(r, c), last)
        return last

    def column(c, rows=range(FBR)):
        return [(r, c) for r in rows]

    def far_side(c):
        @pl.when(has_far)
        def _():
            across_in.wait_recv()
            hold_all(with_side, column(c))

    def even_order(last):
        far_side(0)
        last = gather_all(held, column(0, inner) + column(1, inner), last)
        beside_in.wait_recv()
        hold_all(with_side, column(2, (first, final)))
        last = gather_all(with_side, column(2, inner), last)

        @pl.when(has_above)
        def _():
            down_in.wait_recv()
            hold_all(with_end, [(first, c) for c in range(FBC)])

        last = gather_all(held, [(first, c) for c in range(FBC)], last)
        pl.when(has_below)(up_in.wait_recv)
        return gather_all(with_end, [(final, c) for c in range(FBC)], last)

    def odd_order(last):
        far_side(2)
        last = gather_all(held, column(1, inner) + column(2, inner), last)
        pl.semaphore_wait(barrier, 1)
        beside.start()
        pl.when(has_above)(down_in.wait_recv)
        pl.when(has_below)(up_in.wait_recv)
        hold_all(with_end, [(first, 0), (final, 0)])
        last = gather_all(with_end, [(r, c) for c in (1, 2) for r in (first, final)], last)

        beside_in.wait_recv()
        return gather_all(with_side, column(0), last)

    last = lax.cond(odd == 1, odd_order, even_order, [jnp.int32(0)] * 6)

    def partial_tiles(owner, target):
        for aggregate in range(2):
            total = chain[jnp.where(owner == -1, last[aggregate], jnp.where(owner == 0, last[2 + aggregate], last[4 + aggregate]))]
            for kind in range(3):
                target[3 * aggregate + kind] = total[:, kind * B : (kind + 1) * B].astype(target.dtype)

    def partial(index, target, there):
        return pltpu.make_async_remote_copy(
            src_ref=out_v.at[index], dst_ref=target, send_sem=part_send.at[index], recv_sem=part_recv.at[index],
            device_id=there, device_id_type=MESH)

    to_near_copy = partial(0, near_hbm, (row, near))
    to_far_copy = partial(1, far_hbm, (row, far))
    partial_tiles(near - col, out_v.at[0])
    to_near_copy.start()

    @pl.when(has_far)
    def _():
        partial_tiles(far - col, out_v.at[1])
        to_far_copy.start()

    partial_tiles(0, mine)

    pl.when(has_above)(up.wait_send)
    pl.when(has_below)(down.wait_send)
    pl.when(has_far)(across.wait_send)
    beside.wait_send()
    pl.when(jnp.logical_not(has_far))(fill.wait)
    to_near_copy.wait()
    pl.when(has_far)(to_far_copy.wait)


def body(n_row, n_col, a_tiles, p_tiles, c_slot):
    any_space, hbm = pl.BlockSpec(memory_space=pl.ANY), pl.BlockSpec(memory_space=pltpu.HBM)
    operands = [
        pltpu.with_memory_space_constraint(x, pltpu.HBM) for x in (a_tiles, p_tiles, jnp.swapaxes(c_slot, 3, 4))
    ]
    mine, far, near = pl.pallas_call(
        functools.partial(kernel, n_row, n_col),
        out_shape=[
            jax.ShapeDtypeStruct((CTD, B, B), F32),
            jax.ShapeDtypeStruct((CTD, B, B), BF16),
            jax.ShapeDtypeStruct((CTD, B, B), BF16),
        ],
        in_specs=[hbm, hbm, hbm],
        out_specs=[pl.BlockSpec(memory_space=pltpu.VMEM), any_space, any_space],
        scratch_shapes=[
            pltpu.SMEM((FBR, FBC, KP, KP, 5), jnp.int32),
            pltpu.VMEM((FBR, FBC, 5, B, B), BF16),
            pltpu.VMEM((FBR + 2, FBC + 2, KP, B, B), BF16),
            pltpu.VMEM((FBR, FBC, 5, B, B), F32),
            pltpu.VMEM((FBR, FBC, KP, B, B), BF16),
            pltpu.VMEM((1 + FBR * FBC * KP, B, 3 * B), F32),
            pltpu.VMEM((2, CTD, B, B), BF16),
            pltpu.SemaphoreType.DMA((2 * FBR + 1,)),
            pltpu.SemaphoreType.DMA((4,)),
            pltpu.SemaphoreType.DMA((4,)),
            pltpu.SemaphoreType.DMA((2,)),
            pltpu.SemaphoreType.DMA((2,)),
            pltpu.SemaphoreType.DMA,
        ],
        compiler_params=pltpu.CompilerParams(
            collective_id=0, has_side_effects=True, vmem_limit_bytes=48 * 1024 * 1024),
        name="coarse",
    )(*operands)
    return mine + far.astype(F32) + near.astype(F32)


def solution(mesh):
    spec = P("row", "col", None, None, None)
    return jax.shard_map(
        functools.partial(body, mesh.shape["row"], mesh.shape["col"]), mesh=mesh, in_specs=(spec, spec, spec),
        out_specs=P(("row", "col"), None, None), check_vma=False)
```

```python
import functools

import jax
import jax.numpy as jnp
from jax import lax
from jax.experimental import pallas as pl
from jax.experimental.pallas import tpu as pltpu
from jax.sharding import PartitionSpec as P

MESH = pl.DeviceIdType.MESH
B = 128
KP = 2
FBR = 4
FBC = 3
CTD = 6
SELF, ABOVE, BELOW, LEFT, RIGHT = range(5)
F32, BF16 = jnp.float32, jnp.bfloat16


def kernel(n_row, n_col, a_hbm, p_hbm, slot_hbm, mine, far_hbm, near_hbm, slot, before, a_v, p_v, acc, pt, chain, out_v,
           load_sem, halo_send, halo_recv, part_send, part_recv, fill_sem):
    row, col = lax.axis_index("row"), lax.axis_index("col")
    odd = lax.rem(col, 2)
    far, near = col - 1 + 2 * odd, col + 1 - 2 * odd
    has_above, has_below = row > 0, row < n_row - 1
    has_far = jnp.logical_and(far >= 0, far < n_col)

    barrier = pltpu.get_barrier_semaphore()

    def greet(there):
        pl.semaphore_signal(barrier, inc=1, device_id=there, device_id_type=MESH)

    pl.when(has_above)(lambda: greet((row - 1, col)))
    pl.when(has_below)(lambda: greet((row + 1, col)))
    pl.when(has_far)(lambda: greet((row, far)))

    load_slot = pltpu.make_async_copy(slot_hbm, slot, load_sem.at[2 * FBR])
    load_slot.start()

    def load_p(r):
        return pltpu.make_async_copy(p_hbm.at[r], p_v.at[1 + r, pl.ds(1, FBC)], load_sem.at[FBR + r])

    def load_a(r):
        return pltpu.make_async_copy(a_hbm.at[r], a_v.at[r], load_sem.at[r])

    for r in range(FBR):
        load_p(r).start()
    for r in (1, 2, 0, 3):
        load_a(r).start()

    def halo(index, source, target, there):
        return pltpu.make_async_remote_copy(
            src_ref=source, dst_ref=target, send_sem=halo_send.at[index], recv_sem=halo_recv.at[index],
            device_id=there, device_id_type=MESH)

    rim_above = p_v.at[0, pl.ds(1, FBC)]
    rim_below = p_v.at[FBR + 1, pl.ds(1, FBC)]

    def rim_column(at):
        return p_v.at[pl.ds(1, FBR), at]

    def outgoing(row_at, column_at):
        return (
            halo(0, row_at(0), rim_below, (row - 1, col)),
            halo(1, row_at(FBR - 1), rim_above, (row + 1, col)),
            halo(2, column_at((FBC - 1) * odd), rim_column((FBC + 1) * (1 - odd)), (row, far)),
            halo(3, column_at((FBC - 1) * (1 - odd)), rim_column((FBC + 1) * odd), (row, near)),
        )

    early = outgoing(lambda r: p_hbm.at[r], lambda c: p_hbm.at[:, c])
    loaded = outgoing(lambda r: p_v.at[1 + r, pl.ds(1, FBC)], lambda c: rim_column(1 + c))
    up, down, across, beside = loaded
    up_in = halo(0, p_hbm.at[0], rim_below, (row - 1, col))
    down_in = halo(1, p_hbm.at[0], rim_above, (row + 1, col))
    across_in = halo(2, p_hbm.at[:, 0], rim_column((FBC + 1) * odd), (row, far))
    beside_in = halo(3, p_hbm.at[:, 0], rim_column((FBC + 1) * (1 - odd)), (row, near))

    def meet(copies):
        up, down, across, beside = copies
        count = 1 - odd + has_above.astype(jnp.int32) + has_below.astype(jnp.int32) + has_far.astype(jnp.int32)
        pl.semaphore_wait(barrier, count)
        pl.when(has_above)(up.start)
        pl.when(has_below)(down.start)
        greet((row, near))
        pl.when(has_far)(across.start)
        pl.when(odd == 0)(beside.start)

    pl.when(row != 1)(lambda: meet(early))

    @pl.when(jnp.logical_not(has_above))
    def _():
        rim_above[...] = jnp.zeros(rim_above.shape, BF16)

    @pl.when(jnp.logical_not(has_below))
    def _():
        rim_below[...] = jnp.zeros(rim_below.shape, BF16)

    fill = pltpu.make_async_copy(out_v.at[1], far_hbm, fill_sem)

    @pl.when(jnp.logical_not(has_far))
    def _():
        edge = (FBC + 1) * odd
        for r in range(FBR):
            p_v[1 + r, edge] = jnp.zeros((KP, B, B), BF16)
        out_v[1] = jnp.zeros((CTD, B, B), BF16)
        fill.start()

    chain[0] = jnp.zeros((B, 3 * B), F32)
    first, final = 0, FBR - 1
    inner = range(1, FBR - 1)

    def column(c, rows=range(FBR)):
        return [(r, c) for r in rows]

    def end_of(r):
        return [(r, c) for c in range(FBC)]

    even_blocks = column(0, inner) + column(1, inner) + column(2, inner) + end_of(first) + end_of(final)
    odd_blocks = column(1, inner) + column(2, inner) + column(1, (first, final)) + column(2, (first, final)) + column(0)
    newest = 1 + FBR * FBC * KP

    def find_places(blocks):
        last = [jnp.int32(0)] * 6
        for r, c in blocks:
            for p in range(KP):
                label = slot[r, c, p, p, SELF] - (col - 1) * CTD
                at = 1 + (r * FBC + c) * KP + p
                place = jnp.int32(0)
                for n in range(6):
                    place = jnp.where(label == 3 * n, last[n], place)
                    last[n] = jnp.where(label == 3 * n, at, last[n])
                before[at] = place
        for n in range(6):
            before[newest + n] = last[n]

    load_slot.wait()
    pl.when(odd == 0)(lambda: find_places(even_blocks))
    pl.when(odd == 1)(lambda: find_places(odd_blocks))

    def transpose_row(r, carry):
        load_p(r).wait()
        for c in range(FBC):
            for p in range(KP):
                pt[r, c, p] = p_v[1 + r, 1 + c, p].T
        return carry

    lax.fori_loop(0, FBR, transpose_row, 0)

    def products(r, c, k, rim_r, rim_c):
        right = jnp.concatenate([p_v[rim_r, rim_c, 0], p_v[rim_r, rim_c, 1]], axis=1)
        ap = jnp.dot(a_v[r, c, k], right, preferred_element_type=F32).astype(BF16).astype(F32)
        tiles = [ap[:, :B], ap[:, B:]]
        sums = [tiles[0] + tiles[1]]
        for p in range(KP):
            base = slot[r, c, p, p, SELF]
            for kind in range(2):
                if k is SELF:
                    other = tiles[1 - p] * jnp.where(slot[r, c, p, 1 - p, k] == base + kind, 1.0, 0.0)
                    sums.append(tiles[p] + other if kind == 0 else other)
                    continue
                keep = [jnp.where(slot[r, c, p, q, k] == base + kind, 1.0, 0.0) for q in range(KP)]
                sums.append(tiles[0] * keep[0] + tiles[1] * keep[1])
        return sums

    def add(one, other):
        return [x + y for x, y in zip(one, other)]

    def held(r, c):
        return [acc[r, c, n] for n in range(5)]

    def hold(r, c, sums):
        for n in range(5):
            acc[r, c, n] = sums[n]

    def gather(r, c, sums):
        for p in range(KP):
            first, second = sums[1 + 2 * p], sums[2 + 2 * p]
            kinds = jnp.concatenate([first, second, sums[0] - first - second], axis=1).astype(BF16)
            term = jnp.dot(pt[r, c, p], kinds, preferred_element_type=F32)
            at = 1 + (r * FBC + c) * KP + p
            chain[at] = term + chain[before[at]]

    def interior(r, verticals):
        load_a(r).wait()
        for c in range(FBC):
            sums = products(r, c, SELF, r + 1, c + 1)
            if c > 0:
                sums = add(sums, products(r, c, LEFT, r + 1, c))
            if c < FBC - 1:
                sums = add(sums, products(r, c, RIGHT, r + 1, c + 2))
            for k, rim in verticals:
                sums = add(sums, products(r, c, k, rim, c + 1))
            hold(r, c, sums)

    def inner_interior(r, carry):
        interior(r, ((ABOVE, r), (BELOW, r + 2)))
        return carry

    def outer_interior(i, carry):
        interior((FBR - 1) * i, ((BELOW - i, 2 + i),))
        return carry

    lax.fori_loop(1, FBR - 1, inner_interior, 0)
    pl.when(row == 1)(lambda: meet(loaded))
    lax.fori_loop(0, 2, outer_interior, 0)

    def with_side(r, c):
        k, rim = (LEFT, 0) if c == 0 else (RIGHT, FBC + 1)
        return add(held(r, c), products(r, c, k, r + 1, rim))

    def with_end(r, c):
        k, rim = (ABOVE, 0) if r == first else (BELOW, FBR + 1)
        return add(held(r, c), products(r, c, k, rim, c + 1))

    def hold_all(sums_of, blocks):
        for r, c in blocks:
            hold(r, c, sums_of(r, c))

    def gather_all(sums_of, blocks):
        for r, c in blocks:
            gather(r, c, sums_of(r, c))

    def far_side(c):
        @pl.when(has_far)
        def _():
            across_in.wait_recv()
            hold_all(with_side, column(c))

    def even_order():
        far_side(0)
        gather_all(held, column(0, inner) + column(1, inner))
        beside_in.wait_recv()
        hold_all(with_side, column(2, (first, final)))
        gather_all(with_side, column(2, inner))

        @pl.when(has_above)
        def _():
            down_in.wait_recv()
            hold_all(with_end, end_of(first))

        gather_all(held, end_of(first))
        pl.when(has_below)(up_in.wait_recv)
        gather_all(with_end, end_of(final))

    def odd_order():
        far_side(2)
        gather_all(held, column(1, inner) + column(2, inner))
        pl.semaphore_wait(barrier, 1)
        beside.start()
        pl.when(has_above)(down_in.wait_recv)
        pl.when(has_below)(up_in.wait_recv)
        hold_all(with_end, [(first, 0), (final, 0)])
        gather_all(with_end, column(1, (first, final)) + column(2, (first, final)))
        beside_in.wait_recv()
        gather_all(with_side, column(0))

    pl.when(odd == 0)(even_order)
    pl.when(odd == 1)(odd_order)

    def partial_tiles(owner, target):
        for aggregate in range(2):
            total = chain[jnp.where(owner == -1, before[newest + aggregate], jnp.where(owner == 0, before[newest + 2 + aggregate], before[newest + 4 + aggregate]))]
            for kind in range(3):
                target[3 * aggregate + kind] = total[:, kind * B : (kind + 1) * B].astype(target.dtype)

    def partial(index, target, there):
        return pltpu.make_async_remote_copy(
            src_ref=out_v.at[index], dst_ref=target, send_sem=part_send.at[index], recv_sem=part_recv.at[index],
            device_id=there, device_id_type=MESH)

    to_near_copy = partial(0, near_hbm, (row, near))
    to_far_copy = partial(1, far_hbm, (row, far))
    partial_tiles(near - col, out_v.at[0])
    to_near_copy.start()

    @pl.when(has_far)
    def _():
        partial_tiles(far - col, out_v.at[1])
        to_far_copy.start()

    partial_tiles(0, mine)

    pl.when(has_above)(up.wait_send)
    pl.when(has_below)(down.wait_send)
    pl.when(has_far)(across.wait_send)
    beside.wait_send()
    pl.when(jnp.logical_not(has_far))(fill.wait)
    to_near_copy.wait()
    pl.when(has_far)(to_far_copy.wait)


def body(n_row, n_col, a_tiles, p_tiles, c_slot):
    any_space, hbm = pl.BlockSpec(memory_space=pl.ANY), pl.BlockSpec(memory_space=pltpu.HBM)
    operands = [
        pltpu.with_memory_space_constraint(x, pltpu.HBM) for x in (a_tiles, p_tiles, jnp.swapaxes(c_slot, 3, 4))
    ]
    mine, far, near = pl.pallas_call(
        functools.partial(kernel, n_row, n_col),
        out_shape=[
            jax.ShapeDtypeStruct((CTD, B, B), F32),
            jax.ShapeDtypeStruct((CTD, B, B), BF16),
            jax.ShapeDtypeStruct((CTD, B, B), BF16),
        ],
        in_specs=[hbm, hbm, hbm],
        out_specs=[pl.BlockSpec(memory_space=pltpu.VMEM), any_space, any_space],
        scratch_shapes=[
            pltpu.SMEM((FBR, FBC, KP, KP, 5), jnp.int32),
            pltpu.SMEM((7 + FBR * FBC * KP,), jnp.int32),
            pltpu.VMEM((FBR, FBC, 5, B, B), BF16),
            pltpu.VMEM((FBR + 2, FBC + 2, KP, B, B), BF16),
            pltpu.VMEM((FBR, FBC, 5, B, B), F32),
            pltpu.VMEM((FBR, FBC, KP, B, B), BF16),
            pltpu.VMEM((1 + FBR * FBC * KP, B, 3 * B), F32),
            pltpu.VMEM((2, CTD, B, B), BF16),
            pltpu.SemaphoreType.DMA((2 * FBR + 1,)),
            pltpu.SemaphoreType.DMA((4,)),
            pltpu.SemaphoreType.DMA((4,)),
            pltpu.SemaphoreType.DMA((2,)),
            pltpu.SemaphoreType.DMA((2,)),
            pltpu.SemaphoreType.DMA,
        ],
        compiler_params=pltpu.CompilerParams(
            collective_id=0, has_side_effects=True, vmem_limit_bytes=48 * 1024 * 1024),
        name="coarse",
    )(*operands)
    return mine + far.astype(F32) + near.astype(F32)


def solution(mesh):
    spec = P("row", "col", None, None, None)
    return jax.shard_map(
        functools.partial(body, mesh.shape["row"], mesh.shape["col"]), mesh=mesh, in_specs=(spec, spec, spec),
        out_specs=P(("row", "col"), None, None), check_vma=False)
```

```python
import functools

import jax
import jax.numpy as jnp
from jax import lax
from jax.experimental import pallas as pl
from jax.experimental.pallas import tpu as pltpu
from jax.sharding import PartitionSpec as P

MESH = pl.DeviceIdType.MESH
B = 128
KP = 2
FBR = 4
FBC = 3
CTD = 6
SELF, ABOVE, BELOW, LEFT, RIGHT = range(5)
F32, BF16 = jnp.float32, jnp.bfloat16


def kernel(n_row, n_col, a_hbm, p_hbm, slot_hbm, mine, far_hbm, near_hbm, slot, before, a_v, p_v, acc, pt, chain, out_v,
           load_sem, halo_send, halo_recv, part_send, part_recv, fill_sem):
    row, col = lax.axis_index("row"), lax.axis_index("col")
    odd = lax.rem(col, 2)
    far, near = col - 1 + 2 * odd, col + 1 - 2 * odd
    has_above, has_below = row > 0, row < n_row - 1
    has_far = jnp.logical_and(far >= 0, far < n_col)

    barrier = pltpu.get_barrier_semaphore()

    def greet(there):
        pl.semaphore_signal(barrier, inc=1, device_id=there, device_id_type=MESH)

    pl.when(has_above)(lambda: greet((row - 1, col)))
    pl.when(has_below)(lambda: greet((row + 1, col)))
    pl.when(has_far)(lambda: greet((row, far)))

    load_slot = pltpu.make_async_copy(slot_hbm, slot, load_sem.at[2 * FBR])
    load_slot.start()

    def load_p(r):
        return pltpu.make_async_copy(p_hbm.at[r], p_v.at[1 + r, pl.ds(1, FBC)], load_sem.at[FBR + r])

    def load_a(r):
        return pltpu.make_async_copy(a_hbm.at[r], a_v.at[r], load_sem.at[r])

    for r in range(FBR):
        load_p(r).start()
    for r in (1, 2):
        load_a(r).start()

    def halo(index, source, target, there):
        return pltpu.make_async_remote_copy(
            src_ref=source, dst_ref=target, send_sem=halo_send.at[index], recv_sem=halo_recv.at[index],
            device_id=there, device_id_type=MESH)

    rim_above = p_v.at[0, pl.ds(1, FBC)]
    rim_below = p_v.at[FBR + 1, pl.ds(1, FBC)]

    def rim_column(at):
        return p_v.at[pl.ds(1, FBR), at]

    def outgoing(row_at, column_at):
        return (
            halo(0, row_at(0), rim_below, (row - 1, col)),
            halo(1, row_at(FBR - 1), rim_above, (row + 1, col)),
            halo(2, column_at((FBC - 1) * odd), rim_column((FBC + 1) * (1 - odd)), (row, far)),
            halo(3, column_at((FBC - 1) * (1 - odd)), rim_column((FBC + 1) * odd), (row, near)),
        )

    early = outgoing(lambda r: p_hbm.at[r], lambda c: p_hbm.at[:, c])
    loaded = outgoing(lambda r: p_v.at[1 + r, pl.ds(1, FBC)], lambda c: rim_column(1 + c))
    up, down, across, beside = loaded
    up_in = halo(0, p_hbm.at[0], rim_below, (row - 1, col))
    down_in = halo(1, p_hbm.at[0], rim_above, (row + 1, col))
    across_in = halo(2, p_hbm.at[:, 0], rim_column((FBC + 1) * odd), (row, far))
    beside_in = halo(3, p_hbm.at[:, 0], rim_column((FBC + 1) * (1 - odd)), (row, near))

    def meet(copies):
        up, down, across, beside = copies
        count = 1 - odd + has_above.astype(jnp.int32) + has_below.astype(jnp.int32) + has_far.astype(jnp.int32)
        pl.semaphore_wait(barrier, count)
        pl.when(has_above)(up.start)
        pl.when(has_below)(down.start)
        greet((row, near))
        pl.when(has_far)(across.start)
        pl.when(odd == 0)(beside.start)

    pl.when(row != 1)(lambda: meet(early))

    @pl.when(jnp.logical_not(has_above))
    def _():
        rim_above[...] = jnp.zeros(rim_above.shape, BF16)

    @pl.when(jnp.logical_not(has_below))
    def _():
        rim_below[...] = jnp.zeros(rim_below.shape, BF16)

    fill = pltpu.make_async_copy(out_v.at[1], far_hbm, fill_sem)

    @pl.when(jnp.logical_not(has_far))
    def _():
        edge = (FBC + 1) * odd
        for r in range(FBR):
            p_v[1 + r, edge] = jnp.zeros((KP, B, B), BF16)
        out_v[1] = jnp.zeros((CTD, B, B), BF16)
        fill.start()

    chain[0] = jnp.zeros((B, 3 * B), F32)
    first, final = 0, FBR - 1
    inner = range(1, FBR - 1)

    def column(c, rows=range(FBR)):
        return [(r, c) for r in rows]

    def end_of(r):
        return [(r, c) for c in range(FBC)]

    even_blocks = column(0, inner) + column(1, inner) + column(2, inner) + end_of(first) + end_of(final)
    odd_blocks = column(1, inner) + column(2, inner) + column(1, (first, final)) + column(2, (first, final)) + column(0)
    newest = 1 + FBR * FBC * KP

    def find_places(blocks):
        last = [jnp.int32(0)] * 6
        for r, c in blocks:
            for p in range(KP):
                label = slot[r, c, p, p, SELF] - (col - 1) * CTD
                at = 1 + (r * FBC + c) * KP + p
                place = jnp.int32(0)
                for n in range(6):
                    place = jnp.where(label == 3 * n, last[n], place)
                    last[n] = jnp.where(label == 3 * n, at, last[n])
                before[at] = place
        for n in range(6):
            before[newest + n] = last[n]

    load_slot.wait()
    pl.when(odd == 0)(lambda: find_places(even_blocks))
    pl.when(odd == 1)(lambda: find_places(odd_blocks))

    def transpose_row(r, carry):
        load_p(r).wait()
        for c in range(FBC):
            for p in range(KP):
                pt[r, c, p] = p_v[1 + r, 1 + c, p].T
        return carry

    lax.fori_loop(0, FBR, transpose_row, 0)
    for r in (0, FBR - 1):
        load_a(r).start()

    def products(r, c, k, rim_r, rim_c):
        right = jnp.concatenate([p_v[rim_r, rim_c, 0], p_v[rim_r, rim_c, 1]], axis=1)
        ap = jnp.dot(a_v[r, c, k], right, preferred_element_type=F32).astype(BF16).astype(F32)
        tiles = [ap[:, :B], ap[:, B:]]
        sums = [tiles[0] + tiles[1]]
        for p in range(KP):
            base = slot[r, c, p, p, SELF]
            for kind in range(2):
                if k is SELF:
                    other = tiles[1 - p] * jnp.where(slot[r, c, p, 1 - p, k] == base + kind, 1.0, 0.0)
                    sums.append(tiles[p] + other if kind == 0 else other)
                    continue
                keep = [jnp.where(slot[r, c, p, q, k] == base + kind, 1.0, 0.0) for q in range(KP)]
                sums.append(tiles[0] * keep[0] + tiles[1] * keep[1])
        return sums

    def add(one, other):
        return [x + y for x, y in zip(one, other)]

    def held(r, c):
        return [acc[r, c, n] for n in range(5)]

    def hold(r, c, sums):
        for n in range(5):
            acc[r, c, n] = sums[n]

    def gather(r, c, sums):
        for p in range(KP):
            first, second = sums[1 + 2 * p], sums[2 + 2 * p]
            kinds = jnp.concatenate([first, second, sums[0] - first - second], axis=1).astype(BF16)
            term = jnp.dot(pt[r, c, p], kinds, preferred_element_type=F32)
            at = 1 + (r * FBC + c) * KP + p
            chain[at] = term + chain[before[at]]

    def interior(r, verticals):
        load_a(r).wait()
        for c in range(FBC):
            sums = products(r, c, SELF, r + 1, c + 1)
            if c > 0:
                sums = add(sums, products(r, c, LEFT, r + 1, c))
            if c < FBC - 1:
                sums = add(sums, products(r, c, RIGHT, r + 1, c + 2))
            for k, rim in verticals:
                sums = add(sums, products(r, c, k, rim, c + 1))
            hold(r, c, sums)

    def inner_interior(r, carry):
        interior(r, ((ABOVE, r), (BELOW, r + 2)))
        return carry

    def outer_interior(i, carry):
        interior((FBR - 1) * i, ((BELOW - i, 2 + i),))
        return carry

    lax.fori_loop(1, FBR - 1, inner_interior, 0)
    pl.when(row == 1)(lambda: meet(loaded))
    lax.fori_loop(0, 2, outer_interior, 0)

    def with_side(r, c):
        k, rim = (LEFT, 0) if c == 0 else (RIGHT, FBC + 1)
        return add(held(r, c), products(r, c, k, r + 1, rim))

    def with_end(r, c):
        k, rim = (ABOVE, 0) if r == first else (BELOW, FBR + 1)
        return add(held(r, c), products(r, c, k, rim, c + 1))

    def hold_all(sums_of, blocks):
        for r, c in blocks:
            hold(r, c, sums_of(r, c))

    def gather_all(sums_of, blocks):
        for r, c in blocks:
            gather(r, c, sums_of(r, c))

    def far_side(c):
        @pl.when(has_far)
        def _():
            across_in.wait_recv()
            hold_all(with_side, column(c))

    def even_order():
        far_side(0)
        gather_all(held, column(0, inner) + column(1, inner))
        beside_in.wait_recv()
        hold_all(with_side, column(2, (first, final)))
        gather_all(with_side, column(2, inner))

        @pl.when(has_above)
        def _():
            down_in.wait_recv()
            hold_all(with_end, end_of(first))

        gather_all(held, end_of(first))
        pl.when(has_below)(up_in.wait_recv)
        gather_all(with_end, end_of(final))

    def odd_order():
        far_side(2)
        gather_all(held, column(1, inner) + column(2, inner))
        pl.semaphore_wait(barrier, 1)
        beside.start()
        pl.when(has_above)(down_in.wait_recv)
        pl.when(has_below)(up_in.wait_recv)
        hold_all(with_end, [(first, 0), (final, 0)])
        gather_all(with_end, column(1, (first, final)) + column(2, (first, final)))
        beside_in.wait_recv()
        gather_all(with_side, column(0))

    pl.when(odd == 0)(even_order)
    pl.when(odd == 1)(odd_order)

    def partial_tiles(owner, target):
        for aggregate in range(2):
            total = chain[jnp.where(owner == -1, before[newest + aggregate], jnp.where(owner == 0, before[newest + 2 + aggregate], before[newest + 4 + aggregate]))]
            for kind in range(3):
                target[3 * aggregate + kind] = total[:, kind * B : (kind + 1) * B].astype(target.dtype)

    def partial(index, target, there):
        return pltpu.make_async_remote_copy(
            src_ref=out_v.at[index], dst_ref=target, send_sem=part_send.at[index], recv_sem=part_recv.at[index],
            device_id=there, device_id_type=MESH)

    to_near_copy = partial(0, near_hbm, (row, near))
    to_far_copy = partial(1, far_hbm, (row, far))
    partial_tiles(near - col, out_v.at[0])
    to_near_copy.start()

    @pl.when(has_far)
    def _():
        partial_tiles(far - col, out_v.at[1])
        to_far_copy.start()

    partial_tiles(0, mine)

    pl.when(has_above)(up.wait_send)
    pl.when(has_below)(down.wait_send)
    pl.when(has_far)(across.wait_send)
    beside.wait_send()
    pl.when(jnp.logical_not(has_far))(fill.wait)
    to_near_copy.wait()
    pl.when(has_far)(to_far_copy.wait)


def body(n_row, n_col, a_tiles, p_tiles, c_slot):
    any_space, hbm = pl.BlockSpec(memory_space=pl.ANY), pl.BlockSpec(memory_space=pltpu.HBM)
    operands = [
        pltpu.with_memory_space_constraint(x, pltpu.HBM) for x in (a_tiles, p_tiles, jnp.swapaxes(c_slot, 3, 4))
    ]
    mine, far, near = pl.pallas_call(
        functools.partial(kernel, n_row, n_col),
        out_shape=[
            jax.ShapeDtypeStruct((CTD, B, B), F32),
            jax.ShapeDtypeStruct((CTD, B, B), BF16),
            jax.ShapeDtypeStruct((CTD, B, B), BF16),
        ],
        in_specs=[hbm, hbm, hbm],
        out_specs=[pl.BlockSpec(memory_space=pltpu.VMEM), any_space, any_space],
        scratch_shapes=[
            pltpu.SMEM((FBR, FBC, KP, KP, 5), jnp.int32),
            pltpu.SMEM((7 + FBR * FBC * KP,), jnp.int32),
            pltpu.VMEM((FBR, FBC, 5, B, B), BF16),
            pltpu.VMEM((FBR + 2, FBC + 2, KP, B, B), BF16),
            pltpu.VMEM((FBR, FBC, 5, B, B), F32),
            pltpu.VMEM((FBR, FBC, KP, B, B), BF16),
            pltpu.VMEM((1 + FBR * FBC * KP, B, 3 * B), F32),
            pltpu.VMEM((2, CTD, B, B), BF16),
            pltpu.SemaphoreType.DMA((2 * FBR + 1,)),
            pltpu.SemaphoreType.DMA((4,)),
            pltpu.SemaphoreType.DMA((4,)),
            pltpu.SemaphoreType.DMA((2,)),
            pltpu.SemaphoreType.DMA((2,)),
            pltpu.SemaphoreType.DMA,
        ],
        compiler_params=pltpu.CompilerParams(
            collective_id=0, has_side_effects=True, vmem_limit_bytes=48 * 1024 * 1024),
        name="coarse",
    )(*operands)
    return mine + far.astype(F32) + near.astype(F32)


def solution(mesh):
    spec = P("row", "col", None, None, None)
    return jax.shard_map(
        functools.partial(body, mesh.shape["row"], mesh.shape["col"]), mesh=mesh, in_specs=(spec, spec, spec),
        out_specs=P(("row", "col"), None, None), check_vma=False)
```
